32 devices in a mesh: sub: 8 (over z, x), col: 4 (over y, core).
Axes of the slice: x: 2, y: 2, z: 4, core: 2. Of those that a mesh axis runs over, the one named last changes fastest.
Arguments:
- leaf_basis: bfloat16 [8, 4, 2048, 512], P('sub', 'col'), as said below
- transfers: bfloat16 [8, 4, 3, 512, 512], P('sub', 'col'), as said below
- couplings: bfloat16 [8, 4, 6, 512, 512], P('sub', 'col'), may hold values from -0.25 to 0.25
- partners: int32 [8, 4, 6], P('sub', 'col'), may hold values from 0 to 3
Outputs:
- q_leaf: bfloat16 [8, 4, 2048, 512], P('sub', 'col')
- root_triangle: bfloat16 [8, 4, 512, 512], P('sub', 'col')
- coupled: bfloat16 [8, 4, 6, 512, 512], P('sub', 'col')
The draws below stay inside these ranges and needn't reach their ends.
Inputs may be any that keep to these rules, and one draw needn't show every extreme that they name: partners[s,c,k] names the leaf cluster (s, partners[s,c,k]) as column cluster; entries may repeat. Every transfer matrix is a positive diagonal plus a dense part; transfers[s,c,l] is equal for all s with the same s >> l. `leaf_basis`: every leaf basis has full column rank.
All inputs are finite; a program needn't handle non-finite values.
Results may differ from the reference program's by a relative error of at most 0.0063.
Values may be sent and summed in bfloat16 or wider, within the bound.
A program may use at most 128 MiB of HBM per device.

```python
import jax
import jax.numpy as jnp
import numpy as np
from jax import lax

LEAF = 2048
RANK = 512
SLOTS = 6
LEVELS = 3
SUBS = 8
COLS = 4


def draw_leaf_basis(key, part):
    base_key = jax.random.fold_in(key, 5)
    first_key, second_key = jax.random.split(base_key, 2)
    shape = (SUBS, COLS, LEAF, RANK)
    own = jax.random.normal(first_key, shape, jnp.float32)
    common = jax.random.normal(second_key, (SUBS, COLS, LEAF, 1), jnp.float32)
    mixed = 0.8 * own + 0.6 * common
    mixed = jnp.clip(mixed, -5.0, 5.0)
    return (mixed / jnp.sqrt(1.0 * LEAF)).astype(jnp.bfloat16)


def draw_transfers(key, part):
    identity = jnp.eye(RANK, dtype=jnp.float32)
    levels_list = []
    for level_index in range(LEVELS):
        level_key = jax.random.fold_in(key, 17 + level_index)
        first_key, second_key = jax.random.split(level_key)
        clusters = SUBS >> level_index
        shape = (clusters, COLS, RANK, RANK)
        diagonal = jnp.exp(jax.random.uniform(first_key, (clusters, COLS, RANK), jnp.float32, jnp.log(0.6), jnp.log(1.6)))
        dense = 0.3 * jax.random.normal(second_key, shape, jnp.float32) / jnp.sqrt(1.0 * RANK)
        matrix = dense + diagonal[..., None] * identity
        levels_list.append(jnp.repeat(matrix, 1 << level_index, axis=0))
    return jnp.stack(levels_list, axis=2).astype(jnp.bfloat16)


def touch_ends(array, key, least, high):
    longest = array.shape.index(max(array.shape))
    spots = []
    for shift in (0, 1):
        where = [jax.random.randint(jax.random.fold_in(key, axis), (), 0, length) for axis, length in enumerate(array.shape)]
        where[longest] = (where[longest] + shift) % array.shape[longest]
        spots.append(tuple(where))
    return array.at[spots[0]].set(least).at[spots[1]].set(high)


def level_of(rng, extent, shards, smallest, top_value):
    gain = 1.0
    for dim, blocks in shards:
        steps = jax.random.uniform(jax.random.fold_in(jax.random.fold_in(rng, 6), dim), (blocks,), jnp.float32, smallest / len(shards), top_value / len(shards))
        gain = gain * jnp.repeat(jnp.exp(steps), extent[dim] // blocks).reshape((-1,) + (1,) * (len(extent) - 1 - dim))
    return gain


def normal_values(key, shape, spread, most, shards=(), kind=jnp.bfloat16):
    level = level_of(key, shape, shards, -0.22, 0.18) if shards else 1.0
    result = jax.random.normal(key, shape, jnp.float32) * spread * level
    return jnp.minimum(jnp.maximum(result, -most), most).astype(kind)


def setup_inputs(seed: int = 0) -> dict:
    seeds = jax.random.split(jax.random.key(seed), 5)
    leaf_basis = draw_leaf_basis(jax.random.fold_in(seeds[4], 71), 0)
    transfers = draw_transfers(jax.random.fold_in(seeds[4], 71), 0)
    couplings = normal_values(seeds[2], (SUBS, COLS, SLOTS, RANK, RANK), RANK ** -0.5, 0.25, ((0, 8), (1, 4)))
    partners = touch_ends(jax.random.randint(seeds[3], (SUBS, COLS, SLOTS), 0, COLS), jax.random.fold_in(seeds[3], 1), 0, COLS - 1).astype(jnp.int32)
    return dict(leaf_basis=leaf_basis, transfers=transfers, couplings=couplings, partners=partners)


highest = lax.Precision.HIGHEST

def reference(leaf_basis, transfers, couplings, partners):
    basis_wide = leaf_basis.astype(jnp.float32)
    gram_leaf = jnp.einsum('scia,scib->scab', basis_wide, basis_wide, precision=highest)
    lower_leaf = jnp.linalg.cholesky(gram_leaf)
    q_transposed = lax.linalg.triangular_solve(lower_leaf, jnp.swapaxes(basis_wide, -1, -2), left_side=True, lower=True)
    q_leaf = jnp.swapaxes(q_transposed, -1, -2).astype(jnp.bfloat16)
    triangle = jnp.swapaxes(lower_leaf, -1, -2)
    rounded = triangle.astype(jnp.bfloat16)
    left_product = jnp.einsum('scab,sckbd->sckad', rounded.astype(jnp.float32), couplings.astype(jnp.float32), precision=highest).astype(jnp.bfloat16)
    sub_index = jnp.arange(SUBS, dtype=jnp.int32)[:, None, None]
    chosen = rounded[sub_index, partners]
    coupled = jnp.einsum('sckab,sckdb->sckad', left_product.astype(jnp.float32), chosen.astype(jnp.float32), precision=highest).astype(jnp.bfloat16)
    current = triangle
    for level_index in range(LEVELS):
        flipped = np.arange(SUBS) ^ 1 << level_index
        moved = jnp.einsum('scab,scbd->scad', current, transfers[:, :, level_index].astype(jnp.float32), precision=highest)
        partner_block = moved[flipped]
        gram_matrix = jnp.einsum('scba,scbd->scad', moved, moved, precision=highest) + jnp.einsum('scba,scbd->scad', partner_block, partner_block, precision=highest)
        current = jnp.swapaxes(jnp.linalg.cholesky(gram_matrix), -1, -2)
    root_triangle = current.astype(jnp.bfloat16)
    return (q_leaf, root_triangle, coupled)
```

```python
import functools

import jax
import jax.numpy as jnp
from jax import lax
from jax.experimental import pallas as pl
from jax.experimental.pallas import tpu as pltpu
from jax.sharding import PartitionSpec as P

highest = lax.Precision.HIGHEST
F32 = jnp.float32
BF16 = jnp.bfloat16
LANES = 128
BLOCK = 64
ROWS = 8
CONTRACT_FIRST = (((0,), (0,)), ((), ()))
CONTRACT_LAST = (((1,), (1,)), ((), ()))


def dot_f32(a, b, dims=(((1,), (0,)), ((), ()))):
    return lax.dot_general(a, b, dims, precision=highest, preferred_element_type=F32)


def dot_bf16(a, b, dims=(((1,), (0,)), ((), ()))):
    return lax.dot_general(a, b, dims, preferred_element_type=F32)


def upper_tiles(order):
    count = order // LANES
    return [(i, j) for i in range(count) for j in range(i, count)]


def eliminate(block, offset):
    finished = []
    row_index = lax.broadcasted_iota(jnp.int32, (ROWS, LANES), 0)
    current = block
    for panel in range(BLOCK // ROWS):
        first = offset + panel * ROWS
        top = current[:ROWS]
        rest = current[ROWS:]
        below = rest.shape[0] > 0
        top_columns = [
            jnp.broadcast_to(top[:, first + j : first + j + 1], top.shape) for j in range(ROWS)
        ]
        if below:
            rest_columns = [
                jnp.broadcast_to(rest[:, first + j : first + j + 1], rest.shape)
                for j in range(ROWS)
            ]
        pivots = top_columns[0]
        for j in range(ROWS):
            inverse = 1.0 / top_columns[j][j : j + 1]
            factor = jnp.where(row_index > j, top_columns[j] * inverse, 0.0)
            if j > 0:
                pivots = jnp.where(row_index == j, top_columns[j], pivots)
            pivot_row = top[j : j + 1]
            if below:
                rest_factor = rest_columns[j] * inverse
                rest = rest - rest_factor * pivot_row
            for k in range(j + 1, ROWS):
                value = top_columns[k][j : j + 1]
                top_columns[k] = top_columns[k] - factor * value
                if below:
                    rest_columns[k] = rest_columns[k] - rest_factor * value
            top = top - factor * pivot_row
        finished.append(top * lax.rsqrt(pivots))
        current = rest
    return jnp.concatenate(finished, axis=0)


def factor(work, order, width, emit):
    extra = width > order
    lane = lax.broadcasted_iota(jnp.int32, (BLOCK, LANES), 1)
    row = lax.broadcasted_iota(jnp.int32, (BLOCK, LANES), 0)
    for start in range(0, order, BLOCK):
        base = start // LANES * LANES
        offset = start - base
        other = BLOCK - offset
        head = work[start : start + BLOCK, base : base + LANES]
        own_half = (lane >= offset) & (lane < offset + BLOCK)
        unit = jnp.where(lane == row + other, 1.0, 0.0).astype(F32)
        solved = eliminate(jnp.where(own_half, head, unit), offset)
        inverse = solved[:, other : other + BLOCK]
        end = order + base + LANES if extra else order
        panel = dot_f32(inverse, work[start : start + BLOCK, base:end])
        emit(start, base, panel)
        for low in range(base + offset * 2, order, LANES):
            shift = low - base
            work[low : low + LANES, low:end] -= dot_f32(
                panel[:, shift : shift + LANES], panel[:, shift:], CONTRACT_FIRST
            )


def gram_kernel(basis_ref, transfers_ref, gram_ref, tiles_ref):
    order = gram_ref.shape[0]
    gram_ref[...] = dot_bf16(basis_ref[...], basis_ref[...], CONTRACT_FIRST)
    moved = transfers_ref[0].astype(F32)
    for level in range(1, transfers_ref.shape[0]):
        moved = dot_f32(moved, transfers_ref[level].astype(F32))
    applied = dot_f32(gram_ref[...], moved)
    for index, (i, j) in enumerate(upper_tiles(order)):
        tiles_ref[index * LANES : (index + 1) * LANES, :] = dot_f32(
            moved[:, i * LANES : (i + 1) * LANES],
            applied[:, j * LANES : (j + 1) * LANES],
            CONTRACT_FIRST,
        )


def upper_mask(panel, start, base):
    shape = panel.shape
    lane = lax.broadcasted_iota(jnp.int32, shape, 1) + base
    row = lax.broadcasted_iota(jnp.int32, shape, 0) + start
    return jnp.where(lane >= row, panel, 0.0)


def leaf_kernel(gram_ref, rounded_ref, high_ref, low_ref, work):
    order = gram_ref.shape[0]
    work[:, :order] = gram_ref[...]
    row = lax.broadcasted_iota(jnp.int32, (order, order), 0)
    lane = lax.broadcasted_iota(jnp.int32, (order, order), 1)
    work[:, order:] = jnp.where(row == lane, 1.0, 0.0).astype(F32)
    rounded_ref[...] = jnp.zeros(rounded_ref.shape, BF16)
    high_ref[...] = jnp.zeros(high_ref.shape, BF16)
    low_ref[...] = jnp.zeros(low_ref.shape, BF16)

    def emit(start, base, panel):
        head = upper_mask(panel[:, : order - base], start, base)
        rounded_ref[start : start + BLOCK, base:] = head.astype(BF16)
        inverse = panel[:, order - base :]
        high = inverse.astype(BF16)
        high_ref[start : start + BLOCK, : base + LANES] = high
        low_ref[start : start + BLOCK, : base + LANES] = (inverse - high.astype(F32)).astype(BF16)

    factor(work, order, 2 * order, emit)


def root_kernel(tiles_ref, root_ref, work):
    order = root_ref.shape[0]
    for index, (i, j) in enumerate(upper_tiles(order)):
        work[i * LANES : (i + 1) * LANES, j * LANES : (j + 1) * LANES] = tiles_ref[
            index * LANES : (index + 1) * LANES, :
        ]
    root_ref[...] = jnp.zeros(root_ref.shape, BF16)

    def emit(start, base, panel):
        root_ref[start : start + BLOCK, base:] = upper_mask(panel, start, base).astype(BF16)

    factor(work, order, order, emit)


def basis_kernel(basis_ref, high_ref, low_ref, q_ref):
    block = basis_ref[...]
    q_ref[...] = (
        dot_bf16(block, high_ref[...], CONTRACT_LAST)
        + dot_bf16(block, low_ref[...], CONTRACT_LAST)
    ).astype(BF16)


def coupled_kernel(partners_ref, rounded_ref, block_ref, chosen_ref, out_ref):
    left = dot_bf16(rounded_ref[...], block_ref[0]).astype(BF16)
    out_ref[0] = dot_bf16(left, chosen_ref[0], CONTRACT_LAST).astype(BF16)


def whole(shape):
    return pl.BlockSpec(shape, lambda *_: (0,) * len(shape))


VMEM_SPEC = pl.BlockSpec(memory_space=pltpu.VMEM)
BIG = pltpu.CompilerParams(vmem_limit_bytes=48 * 1024 * 1024)


def cost(flops, size):
    return pl.CostEstimate(flops=flops, bytes_accessed=size, transcendentals=0)


def sum_group(value, levels):
    count = lax.axis_size("sub")
    size = 1 << levels
    groups = [list(range(low, low + size)) for low in range(0, count, size)]
    if len(groups) == 1:
        return lax.psum(value, "sub")
    return lax.psum(value, "sub", axis_index_groups=groups)


def shards(leaf_basis, transfers, couplings, partners):
    basis, level_transfers = leaf_basis[0, 0], transfers[0, 0]
    blocks, slots = couplings[0, 0], partners[0, 0]
    leaf, order = basis.shape
    levels = level_transfers.shape[0]
    tile_count = len(upper_tiles(order))
    square = (order, order)
    cube = order * order * order
    gram, tiles = pl.pallas_call(
        gram_kernel,
        out_shape=(
            jax.ShapeDtypeStruct(square, F32),
            jax.ShapeDtypeStruct((tile_count * LANES, LANES), F32),
        ),
        in_specs=[VMEM_SPEC] * 2,
        out_specs=(VMEM_SPEC, VMEM_SPEC),
        compiler_params=BIG,
        cost_estimate=cost(2 * cube * 24, leaf * order * 2),
        name="gram",
    )(basis, level_transfers)
    root_tiles = sum_group(tiles, levels)
    rounded, high, low = pl.pallas_call(
        leaf_kernel,
        out_shape=tuple(jax.ShapeDtypeStruct(square, BF16) for _ in range(3)),
        in_specs=[VMEM_SPEC],
        out_specs=(VMEM_SPEC,) * 3,
        scratch_shapes=[pltpu.VMEM((order, 2 * order), F32)],
        compiler_params=BIG,
        cost_estimate=cost(2 * cube * 100, 4 * order * order),
        name="leaf_factor",
    )(gram)
    gathered = lax.all_gather(rounded, "col", axis=0, tiled=False)
    chunk = leaf // 4
    q_leaf = pl.pallas_call(
        basis_kernel,
        grid=(leaf // chunk,),
        out_shape=jax.ShapeDtypeStruct((leaf, order), BF16),
        in_specs=[pl.BlockSpec((chunk, order), lambda i: (i, 0)), whole(square), whole(square)],
        out_specs=pl.BlockSpec((chunk, order), lambda i: (i, 0)),
        compiler_params=BIG,
        cost_estimate=cost(4 * leaf * order * order, leaf * order * 4),
        name="basis",
    )(basis, high, low)
    slot_count = blocks.shape[0]
    one = (1, order, order)
    coupled = pl.pallas_call(
        coupled_kernel,
        grid_spec=pltpu.PrefetchScalarGridSpec(
            num_scalar_prefetch=1,
            grid=(slot_count,),
            in_specs=[
                pl.BlockSpec(square, lambda k, p: (0, 0)),
                pl.BlockSpec(one, lambda k, p: (k, 0, 0)),
                pl.BlockSpec(one, lambda k, p: (p[k], 0, 0)),
            ],
            out_specs=pl.BlockSpec(one, lambda k, p: (k, 0, 0)),
        ),
        out_shape=jax.ShapeDtypeStruct(blocks.shape, BF16),
        compiler_params=BIG,
        cost_estimate=cost(4 * cube * slot_count, slot_count * order * order * 6),
        name="coupled",
    )(slots, rounded, blocks, gathered)
    root = pl.pallas_call(
        root_kernel,
        out_shape=jax.ShapeDtypeStruct(square, BF16),
        in_specs=[VMEM_SPEC],
        out_specs=VMEM_SPEC,
        scratch_shapes=[pltpu.VMEM(square, F32)],
        compiler_params=BIG,
        cost_estimate=cost(2 * cube * 100, 4 * order * order),
        name="root_factor",
    )(root_tiles)
    return (q_leaf[None, None], root[None, None], coupled[None, None])


def solution(mesh):
    in_specs = (
        P("sub", "col", None, None),
        P("sub", "col", None, None, None),
        P("sub", "col", None, None, None),
        P("sub", "col", None),
    )
    out_specs = (
        P("sub", "col", None, None),
        P("sub", "col", None, None),
        P("sub", "col", None, None, None),
    )
    return jax.shard_map(shards, mesh=mesh, in_specs=in_specs, out_specs=out_specs, check_vma=False)
```

```python
import functools

import jax
import jax.numpy as jnp
from jax import lax
from jax.experimental import pallas as pl
from jax.experimental.pallas import tpu as pltpu
from jax.sharding import PartitionSpec as P

highest = lax.Precision.HIGHEST
F32 = jnp.float32
BF16 = jnp.bfloat16
LANES = 128
BLOCK = 64
ROWS = 8
SUM_AT = 4
MESH = pl.DeviceIdType.MESH
CONTRACT_FIRST = (((0,), (0,)), ((), ()))
CONTRACT_LAST = (((1,), (1,)), ((), ()))


def dot_f32(a, b, dims=(((1,), (0,)), ((), ()))):
    return lax.dot_general(a, b, dims, precision=highest, preferred_element_type=F32)


def dot_bf16(a, b, dims=(((1,), (0,)), ((), ()))):
    return lax.dot_general(a, b, dims, preferred_element_type=F32)


def upper_tiles(order):
    count = order // LANES
    return [(i, j) for i in range(count) for j in range(i, count)]


def eliminate(block, offset):
    finished = []
    row_index = lax.broadcasted_iota(jnp.int32, (ROWS, LANES), 0)

    def spread(part, first):
        columns = [part[:, first + j : first + j + 1] for j in range(ROWS)]
        return jnp.stack([jnp.broadcast_to(column, part.shape) for column in columns])

    current = block
    for panel in range(BLOCK // ROWS):
        first = offset + panel * ROWS
        top, rest = current[:ROWS], current[ROWS:]
        below = rest.shape[0] > 0
        top_columns = spread(top, first)
        if below:
            rest_columns = spread(rest, first)
        pivots = top_columns[0]
        for j in range(ROWS):
            lead = top_columns[0]
            if j > 0:
                pivots = jnp.where(row_index == j, lead, pivots)
            inverse = 1.0 / lead[j : j + 1]
            factor = jnp.where(row_index > j, lead * inverse, 0.0)
            pivot_row = top[j : j + 1]
            if below:
                rest_factor = rest_columns[0] * inverse
                rest = rest - rest_factor * pivot_row
            if j + 1 < ROWS:
                later = top_columns[1:]
                values = later[:, j : j + 1]
                top_columns = later - factor[None] * values
                if below:
                    rest_columns = rest_columns[1:] - rest_factor[None] * values
                top = top - factor * pivot_row
        finished.append(top * lax.rsqrt(pivots))
        current = rest
    return jnp.concatenate(finished, axis=0)


def factor(work, order, width, emit, between=None):
    extra = width > order
    lane = lax.broadcasted_iota(jnp.int32, (BLOCK, LANES), 1)
    row = lax.broadcasted_iota(jnp.int32, (BLOCK, LANES), 0)
    for start in range(0, order, BLOCK):
        base = start // LANES * LANES
        offset = start - base
        other = BLOCK - offset
        head = work[start : start + BLOCK, base : base + LANES]
        own_half = (lane >= offset) & (lane < offset + BLOCK)
        unit = jnp.where(lane == row + other, 1.0, 0.0).astype(F32)
        solved = eliminate(jnp.where(own_half, head, unit), offset)
        inverse = solved[:, other : other + BLOCK]
        end = order + base + LANES if extra else order
        panel = dot_f32(inverse, work[start : start + BLOCK, base:end])
        emit(start, base, panel)
        if between is not None:
            between(start // BLOCK)
        for low in range(base + offset * 2, order, LANES):
            shift = low - base
            work[low : low + LANES, low:end] -= dot_f32(
                panel[:, shift : shift + LANES], panel[:, shift:], CONTRACT_FIRST
            )


def dot_exact(a, b):
    high = a.astype(BF16)
    left = a - high.astype(F32)
    middle = left.astype(BF16)
    low = (left - middle.astype(F32)).astype(BF16)
    return dot_bf16(high, b) + (dot_bf16(middle, b) + dot_bf16(low, b))


def projected_gram(gram_ref, transfers_ref, tiles_ref, order):
    moved = dot_bf16(transfers_ref[0], transfers_ref[1]) if transfers_ref.shape[0] > 1 else (
        transfers_ref[0].astype(F32)
    )
    for level in range(2, transfers_ref.shape[0]):
        moved = dot_exact(moved, transfers_ref[level])
    applied = dot_f32(gram_ref[...], moved)
    for index, (i, j) in enumerate(upper_tiles(order)):
        tiles_ref[index * LANES : (index + 1) * LANES, :] = dot_f32(
            moved[:, i * LANES : (i + 1) * LANES],
            applied[:, j * LANES : (j + 1) * LANES],
            CONTRACT_FIRST,
        )


def upper_mask(panel, start, base):
    shape = panel.shape
    lane = lax.broadcasted_iota(jnp.int32, shape, 1) + base
    row = lax.broadcasted_iota(jnp.int32, shape, 0) + start
    return jnp.where(lane >= row, panel, 0.0)


def tree_kernel(
    group,
    basis_ref,
    transfers_ref,
    gathered_ref,
    high_ref,
    low_ref,
    root_ref,
    basis,
    level_transfers,
    work,
    tiles,
    arrived,
    total,
    load_sem,
    sum_send,
    sum_recv,
    back_send,
    back_recv,
    col_send,
    col_recv,
):
    order = root_ref.shape[0]
    cols = gathered_ref.shape[0]
    share = arrived.shape[1]
    sub, col = lax.axis_index("sub"), lax.axis_index("col")
    rank = lax.rem(sub, group)
    group_start = sub - rank

    loads = [
        pltpu.make_async_copy(basis_ref, basis, load_sem.at[0]),
        pltpu.make_async_copy(transfers_ref, level_transfers, load_sem.at[1]),
    ]
    for load in loads:
        load.start()

    def sub_peer(step):
        return group_start + lax.rem(rank + step, group)

    def col_peer(step):
        return lax.rem(col + step, cols)

    barrier = pltpu.get_barrier_semaphore()
    for step in range(1, group):
        pl.semaphore_signal(barrier, inc=1, device_id=(sub_peer(step), col), device_id_type=MESH)
    for step in range(1, cols):
        pl.semaphore_signal(barrier, inc=1, device_id=(sub, col_peer(step)), device_id_type=MESH)
    pl.semaphore_wait(barrier, group - 1 + cols - 1)

    row = lax.broadcasted_iota(jnp.int32, (order, order), 0)
    lane = lax.broadcasted_iota(jnp.int32, (order, order), 1)
    loads[0].wait()
    work[:, :order] = dot_bf16(basis[...], basis[...], CONTRACT_FIRST)
    work[:, order:] = jnp.where(row == lane, 1.0, 0.0).astype(F32)
    loads[1].wait()
    used = len(upper_tiles(order)) * LANES
    if tiles.shape[0] > used:
        tiles[used:, :] = jnp.zeros((tiles.shape[0] - used, LANES), F32)
    projected_gram(work.at[:, :order], level_transfers, tiles, order)

    def rows_of(member):
        return pl.ds(pl.multiple_of(member * share, ROWS), share)

    sums = [
        pltpu.make_async_remote_copy(
            src_ref=tiles.at[rows_of(lax.rem(rank + step, group))],
            dst_ref=arrived.at[step - 1],
            send_sem=sum_send.at[step - 1],
            recv_sem=sum_recv.at[step - 1],
            device_id=(sub_peer(step), col),
            device_id_type=MESH,
        )
        for step in range(1, group)
    ]
    for copy in sums:
        copy.start()
    returns = [
        pltpu.make_async_remote_copy(
            src_ref=total.at[rows_of(rank)],
            dst_ref=total.at[rows_of(rank)],
            send_sem=back_send.at[step - 1],
            recv_sem=back_recv.at[step - 1],
            device_id=(sub_peer(step), col),
            device_id_type=MESH,
        )
        for step in range(1, group)
    ]

    def between(index):
        if index == SUM_AT:
            value = tiles[rows_of(rank), :]
            for step in range(1, group):
                sums[step - 1].wait_recv()
                value = value + arrived[step - 1]
            total[rows_of(rank), :] = value
            for copy in returns:
                copy.start()

    own = gathered_ref.at[col]
    own[...] = jnp.zeros((order, order), BF16)
    high_ref[...] = jnp.zeros(high_ref.shape, BF16)
    low_ref[...] = jnp.zeros(low_ref.shape, BF16)

    def emit_leaf(start, base, panel):
        head = upper_mask(panel[:, : order - base], start, base)
        own[start : start + BLOCK, base:] = head.astype(BF16)
        inverse = panel[:, order - base :]
        high = inverse.astype(BF16)
        high_ref[start : start + BLOCK, : base + LANES] = high
        low_ref[start : start + BLOCK, : base + LANES] = (inverse - high.astype(F32)).astype(BF16)

    factor(work, order, 2 * order, emit_leaf, between)

    shown = [
        pltpu.make_async_remote_copy(
            src_ref=gathered_ref.at[col],
            dst_ref=gathered_ref.at[col],
            send_sem=col_send.at[step - 1],
            recv_sem=col_recv.at[step - 1],
            device_id=(sub, col_peer(step)),
            device_id_type=MESH,
        )
        for step in range(1, cols)
    ]
    for copy in returns:
        copy.wait_recv()
    for copy in shown:
        copy.start()

    for index, (i, j) in enumerate(upper_tiles(order)):
        work[i * LANES : (i + 1) * LANES, j * LANES : (j + 1) * LANES] = total[
            index * LANES : (index + 1) * LANES, :
        ]
    root_ref[...] = jnp.zeros(root_ref.shape, BF16)

    def emit_root(start, base, panel):
        root_ref[start : start + BLOCK, base:] = upper_mask(panel, start, base).astype(BF16)

    factor(work, order, order, emit_root)
    for copy in shown:
        copy.wait()
    for copy in sums + returns:
        copy.wait_send()


def basis_kernel(basis_ref, high_ref, low_ref, q_ref):
    block = basis_ref[...]
    q_ref[...] = (
        dot_bf16(block, high_ref[...], CONTRACT_LAST)
        + dot_bf16(block, low_ref[...], CONTRACT_LAST)
    ).astype(BF16)


def coupled_kernel(partners_ref, rounded_ref, block_ref, chosen_ref, out_ref):
    left = dot_bf16(rounded_ref[0], block_ref[0]).astype(BF16)
    out_ref[0] = dot_bf16(left, chosen_ref[0], CONTRACT_LAST).astype(BF16)


def whole(shape):
    return pl.BlockSpec(shape, lambda *_: (0,) * len(shape))


VMEM_SPEC = pl.BlockSpec(memory_space=pltpu.VMEM)
BIG = pltpu.CompilerParams(vmem_limit_bytes=48 * 1024 * 1024)


def cost(flops, size):
    return pl.CostEstimate(flops=flops, bytes_accessed=size, transcendentals=0)


def shards(leaf_basis, transfers, couplings, partners):
    basis, level_transfers = leaf_basis[0, 0], transfers[0, 0]
    blocks, slots = couplings[0, 0], partners[0, 0]
    leaf, order = basis.shape
    levels = level_transfers.shape[0]
    group = min(1 << levels, lax.axis_size("sub"))
    cols = lax.axis_size("col")
    rows = len(upper_tiles(order)) * LANES
    share = -(-rows // (group * ROWS)) * ROWS
    square = (order, order)
    cube = order * order * order
    pair = max(group - 1, 1)
    across = max(cols - 1, 1)
    gathered, high, low, root = pl.pallas_call(
        functools.partial(tree_kernel, group),
        out_shape=(
            jax.ShapeDtypeStruct((cols,) + square, BF16),
            jax.ShapeDtypeStruct(square, BF16),
            jax.ShapeDtypeStruct(square, BF16),
            jax.ShapeDtypeStruct(square, BF16),
        ),
        in_specs=[pl.BlockSpec(memory_space=pl.ANY)] * 2,
        out_specs=(VMEM_SPEC,) * 4,
        scratch_shapes=[
            pltpu.VMEM(basis.shape, BF16),
            pltpu.VMEM(level_transfers.shape, BF16),
            pltpu.VMEM((order, 2 * order), F32),
            pltpu.VMEM((group * share, LANES), F32),
            pltpu.VMEM((pair, share, LANES), F32),
            pltpu.VMEM((group * share, LANES), F32),
            pltpu.SemaphoreType.DMA((2,)),
            pltpu.SemaphoreType.DMA((pair,)),
            pltpu.SemaphoreType.DMA((pair,)),
            pltpu.SemaphoreType.DMA((pair,)),
            pltpu.SemaphoreType.DMA((pair,)),
            pltpu.SemaphoreType.DMA((across,)),
            pltpu.SemaphoreType.DMA((across,)),
        ],
        compiler_params=pltpu.CompilerParams(
            vmem_limit_bytes=56 * 1024 * 1024, collective_id=0, has_side_effects=True
        ),
        cost_estimate=cost(2 * cube * 200, 4 * leaf * order),
        name="tree",
    )(basis, level_transfers)
    own_slot = lax.axis_index("col").astype(jnp.int32)
    places = jnp.concatenate([slots, own_slot[None]])
    chunk = leaf // 4
    q_leaf = pl.pallas_call(
        basis_kernel,
        grid=(leaf // chunk,),
        out_shape=jax.ShapeDtypeStruct((leaf, order), BF16),
        in_specs=[pl.BlockSpec((chunk, order), lambda i: (i, 0)), whole(square), whole(square)],
        out_specs=pl.BlockSpec((chunk, order), lambda i: (i, 0)),
        compiler_params=BIG,
        cost_estimate=cost(4 * leaf * order * order, leaf * order * 4),
        name="basis",
    )(basis, high, low)
    slot_count = blocks.shape[0]
    one = (1, order, order)
    coupled = pl.pallas_call(
        coupled_kernel,
        grid_spec=pltpu.PrefetchScalarGridSpec(
            num_scalar_prefetch=1,
            grid=(slot_count,),
            in_specs=[
                pl.BlockSpec(one, lambda k, p: (p[slot_count], 0, 0)),
                pl.BlockSpec(one, lambda k, p: (k, 0, 0)),
                pl.BlockSpec(one, lambda k, p: (p[k], 0, 0)),
            ],
            out_specs=pl.BlockSpec(one, lambda k, p: (k, 0, 0)),
        ),
        out_shape=jax.ShapeDtypeStruct(blocks.shape, BF16),
        compiler_params=BIG,
        cost_estimate=cost(4 * cube * slot_count, slot_count * order * order * 6),
        name="coupled",
    )(places, gathered, blocks, gathered)
    return (q_leaf[None, None], root[None, None], coupled[None, None])


def solution(mesh):
    in_specs = (
        P("sub", "col", None, None),
        P("sub", "col", None, None, None),
        P("sub", "col", None, None, None),
        P("sub", "col", None),
    )
    out_specs = (
        P("sub", "col", None, None),
        P("sub", "col", None, None),
        P("sub", "col", None, None, None),
    )
    return jax.shard_map(shards, mesh=mesh, in_specs=in_specs, out_specs=out_specs, check_vma=False)
```

```python
import functools

import jax
import jax.numpy as jnp
from jax import lax
from jax.experimental import pallas as pl
from jax.experimental.pallas import tpu as pltpu
from jax.sharding import PartitionSpec as P

highest = lax.Precision.HIGHEST
F32 = jnp.float32
BF16 = jnp.bfloat16
LANES = 128
BLOCK = 64
ROWS = 8
SUM_BEFORE = 2
MESH = pl.DeviceIdType.MESH
CONTRACT_FIRST = (((0,), (0,)), ((), ()))
CONTRACT_LAST = (((1,), (1,)), ((), ()))


def dot_f32(a, b, dims=(((1,), (0,)), ((), ()))):
    return lax.dot_general(a, b, dims, precision=highest, preferred_element_type=F32)


def dot_bf16(a, b, dims=(((1,), (0,)), ((), ()))):
    return lax.dot_general(a, b, dims, preferred_element_type=F32)


def upper_tiles(order):
    count = order // LANES
    return [(i, j) for i in range(count) for j in range(i, count)]


def eliminate(block, offset):
    finished = []
    row_index = lax.broadcasted_iota(jnp.int32, (ROWS, LANES), 0)

    def spread(part, first):
        columns = [part[:, first + j : first + j + 1] for j in range(ROWS)]
        return jnp.stack([jnp.broadcast_to(column, part.shape) for column in columns])

    current = block
    for panel in range(BLOCK // ROWS):
        first = offset + panel * ROWS
        top, rest = current[:ROWS], current[ROWS:]
        below = rest.shape[0] > 0
        top_columns = spread(top, first)
        if below:
            rest_columns = spread(rest, first)
        pivots = top_columns[0]
        for j in range(ROWS):
            lead = top_columns[0]
            if j > 0:
                pivots = jnp.where(row_index == j, lead, pivots)
            inverse = pl.reciprocal(lead[j : j + 1], approx=True)
            factor = jnp.where(row_index > j, lead, 0.0) * inverse
            pivot_row = top[j : j + 1]
            if below:
                rest_factor = rest_columns[0] * inverse
                rest = rest - rest_factor * pivot_row
            if j + 1 < ROWS:
                later = top_columns[1:]
                values = later[:, j : j + 1]
                top_columns = later - factor[None] * values
                if below:
                    rest_columns = rest_columns[1:] - rest_factor[None] * values
                top = top - factor * pivot_row
        finished.append(top * lax.rsqrt(pivots))
        current = rest
    return jnp.concatenate(finished, axis=0)


def factor(work, order, width, emit, between=None):
    extra = width > order
    lane = lax.broadcasted_iota(jnp.int32, (BLOCK, LANES), 1)
    row = lax.broadcasted_iota(jnp.int32, (BLOCK, LANES), 0)
    head = work[:BLOCK, :LANES]
    for start in range(0, order, BLOCK):
        base = start // LANES * LANES
        offset = start - base
        other = BLOCK - offset
        own_half = (lane >= offset) & (lane < offset + BLOCK)
        unit = jnp.where(lane == row + other, 1.0, 0.0).astype(F32)
        solved = eliminate(jnp.where(own_half, head, unit), offset)
        inverse = solved[:, other : other + BLOCK]
        following = start + BLOCK
        if following < order:
            ahead = following // LANES * LANES
            near = dot_f32(inverse, work[start:following, ahead : ahead + LANES])
            shift = following - ahead
            head = work[following : following + BLOCK, ahead : ahead + LANES] - dot_f32(
                near[:, shift : shift + BLOCK], near, CONTRACT_FIRST
            )
        end = order + base + LANES if extra else order
        panel = dot_f32(inverse, work[start:following, base:end])
        emit(start, base, panel)
        if between is not None:
            between(start // BLOCK)
        for low in range(base + offset * 2, order, LANES):
            shift = low - base
            work[low : low + LANES, low:end] -= dot_f32(
                panel[:, shift : shift + LANES], panel[:, shift:], CONTRACT_FIRST
            )


def parts_of(a):
    high = a.astype(BF16)
    left = a - high.astype(F32)
    middle = left.astype(BF16)
    return high, middle, (left - middle.astype(F32)).astype(BF16)


def projected_gram(gram_ref, transfers_ref, tiles_ref, order):
    current = gram_ref[...]
    levels = transfers_ref.shape[0]
    for level in range(levels):
        transfer = transfers_ref[level]
        high, middle, low = parts_of(current)
        applied = dot_bf16(high, transfer) + (
            dot_bf16(middle, transfer) + dot_bf16(low, transfer)
        )
        high, middle, low = parts_of(applied)
        if level + 1 < levels:
            current = dot_bf16(transfer, high, CONTRACT_FIRST) + (
                dot_bf16(transfer, middle, CONTRACT_FIRST)
                + dot_bf16(transfer, low, CONTRACT_FIRST)
            )
    start = 0
    for first in range(0, order, LANES):
        left = transfers_ref[levels - 1, :, first : first + LANES]
        strip = dot_bf16(left, high[:, first:], CONTRACT_FIRST) + (
            dot_bf16(left, middle[:, first:], CONTRACT_FIRST)
            + dot_bf16(left, low[:, first:], CONTRACT_FIRST)
        )
        for column in range(0, order - first, LANES):
            tiles_ref[start : start + LANES, :] = strip[:, column : column + LANES]
            start += LANES


def upper_mask(panel, start, base):
    shape = panel.shape
    lane = lax.broadcasted_iota(jnp.int32, shape, 1) + base
    row = lax.broadcasted_iota(jnp.int32, shape, 0) + start
    return jnp.where(lane >= row, panel, 0.0)


def tree_kernel(
    group,
    basis_ref,
    transfers_ref,
    blocks_ref,
    gathered_ref,
    q_ref,
    left_ref,
    root_ref,
    basis,
    level_transfers,
    blocks,
    high_ref,
    low_ref,
    work,
    tiles,
    arrived,
    total,
    load_sem,
    sum_send,
    sum_recv,
    back_send,
    back_recv,
    col_send,
    col_recv,
):
    order = root_ref.shape[0]
    cols = gathered_ref.shape[0]
    share = arrived.shape[1]
    sub, col = lax.axis_index("sub"), lax.axis_index("col")
    rank = lax.rem(sub, group)
    group_start = sub - rank

    loads = [
        pltpu.make_async_copy(basis_ref, basis, load_sem.at[0]),
        pltpu.make_async_copy(transfers_ref, level_transfers, load_sem.at[1]),
        pltpu.make_async_copy(blocks_ref, blocks, load_sem.at[2]),
    ]
    for load in loads:
        load.start()

    def sub_peer(step):
        return group_start + lax.rem(rank + step, group)

    def col_peer(step):
        return lax.rem(col + step, cols)

    barrier = pltpu.get_barrier_semaphore()
    for step in range(1, group):
        pl.semaphore_signal(barrier, inc=1, device_id=(sub_peer(step), col), device_id_type=MESH)
    for step in range(1, cols):
        pl.semaphore_signal(barrier, inc=1, device_id=(sub, col_peer(step)), device_id_type=MESH)
    pl.semaphore_wait(barrier, group - 1 + cols - 1)

    row = lax.broadcasted_iota(jnp.int32, (order, order), 0)
    lane = lax.broadcasted_iota(jnp.int32, (order, order), 1)
    loads[0].wait()
    work[:, :order] = dot_bf16(basis[...], basis[...], CONTRACT_FIRST)
    work[:, order:] = jnp.where(row == lane, 1.0, 0.0).astype(F32)
    loads[1].wait()
    used = len(upper_tiles(order)) * LANES
    if tiles.shape[0] > used:
        tiles[used:, :] = jnp.zeros((tiles.shape[0] - used, LANES), F32)
    projected_gram(work.at[:, :order], level_transfers, tiles, order)

    def rows_of(member):
        return pl.ds(pl.multiple_of(member * share, ROWS), share)

    sums = [
        pltpu.make_async_remote_copy(
            src_ref=tiles.at[rows_of(lax.rem(rank + step, group))],
            dst_ref=arrived.at[step - 1],
            send_sem=sum_send.at[step - 1],
            recv_sem=sum_recv.at[step - 1],
            device_id=(sub_peer(step), col),
            device_id_type=MESH,
        )
        for step in range(1, group)
    ]
    for copy in sums:
        copy.start()
    returns = [
        pltpu.make_async_remote_copy(
            src_ref=total.at[rows_of(rank)],
            dst_ref=total.at[rows_of(rank)],
            send_sem=back_send.at[step - 1],
            recv_sem=back_recv.at[step - 1],
            device_id=(sub_peer(step), col),
            device_id_type=MESH,
        )
        for step in range(1, group)
    ]

    half = order // 2
    shown = [
        pltpu.make_async_remote_copy(
            src_ref=gathered_ref.at[col, pl.ds(part * half, half)],
            dst_ref=gathered_ref.at[col, pl.ds(part * half, half)],
            send_sem=col_send.at[part, step - 1],
            recv_sem=col_recv.at[part, step - 1],
            device_id=(sub, col_peer(step)),
            device_id_type=MESH,
        )
        for part in range(2)
        for step in range(1, cols)
    ]
    early, late = shown[: cols - 1], shown[cols - 1 :]

    def between(index):
        if (index + 1) * BLOCK == half:
            for copy in early:
                copy.start()
        if (index + 1) * BLOCK == order - SUM_BEFORE * BLOCK:
            value = tiles[rows_of(rank), :]
            for step in range(1, group):
                sums[step - 1].wait_recv()
                value = value + arrived[step - 1]
            total[rows_of(rank), :] = value
            for copy in returns:
                copy.start()

    own = gathered_ref.at[col]
    own[...] = jnp.zeros((order, order), BF16)
    high_ref[...] = jnp.zeros(high_ref.shape, BF16)
    low_ref[...] = jnp.zeros(low_ref.shape, BF16)

    def emit_leaf(start, base, panel):
        head = upper_mask(panel[:, : order - base], start, base)
        own[start : start + BLOCK, base:] = head.astype(BF16)
        inverse = panel[:, order - base :]
        high = inverse.astype(BF16)
        high_ref[start : start + BLOCK, : base + LANES] = high
        low_ref[start : start + BLOCK, : base + LANES] = (inverse - high.astype(F32)).astype(BF16)

    factor(work, order, 2 * order, emit_leaf, between)

    for copy in late:
        copy.start()
    chunk = order
    for low in range(0, basis.shape[0], chunk):
        rows = basis[low : low + chunk, :]
        q_ref[low : low + chunk, :] = (
            dot_bf16(rows, high_ref[...], CONTRACT_LAST)
            + dot_bf16(rows, low_ref[...], CONTRACT_LAST)
        ).astype(BF16)
    loads[2].wait()
    rounded = own[...]
    for slot in range(blocks.shape[0]):
        left_ref[slot] = dot_bf16(rounded, blocks[slot]).astype(BF16)
    for copy in returns:
        copy.wait_recv()

    for index, (i, j) in enumerate(upper_tiles(order)):
        work[i * LANES : (i + 1) * LANES, j * LANES : (j + 1) * LANES] = total[
            index * LANES : (index + 1) * LANES, :
        ]
    root_ref[...] = jnp.zeros(root_ref.shape, BF16)

    def emit_root(start, base, panel):
        root_ref[start : start + BLOCK, base:] = upper_mask(panel, start, base).astype(BF16)

    factor(work, order, order, emit_root)
    for copy in shown:
        copy.wait()
    for copy in sums + returns:
        copy.wait_send()


def coupled_kernel(partners_ref, left_ref, chosen_ref, out_ref):
    out_ref[0] = dot_bf16(left_ref[0], chosen_ref[0], CONTRACT_LAST).astype(BF16)


VMEM_SPEC = pl.BlockSpec(memory_space=pltpu.VMEM)
BIG = pltpu.CompilerParams(vmem_limit_bytes=48 * 1024 * 1024)


def cost(flops, size):
    return pl.CostEstimate(flops=flops, bytes_accessed=size, transcendentals=0)


def shards(leaf_basis, transfers, couplings, partners):
    basis, level_transfers = leaf_basis[0, 0], transfers[0, 0]
    blocks, slots = couplings[0, 0], partners[0, 0]
    leaf, order = basis.shape
    levels = level_transfers.shape[0]
    group = min(1 << levels, lax.axis_size("sub"))
    cols = lax.axis_size("col")
    rows = len(upper_tiles(order)) * LANES
    share = -(-rows // (group * ROWS)) * ROWS
    square = (order, order)
    cube = order * order * order
    pair = max(group - 1, 1)
    across = max(cols - 1, 1)
    gathered, q_leaf, left, root = pl.pallas_call(
        functools.partial(tree_kernel, group),
        out_shape=(
            jax.ShapeDtypeStruct((cols,) + square, BF16),
            jax.ShapeDtypeStruct(basis.shape, BF16),
            jax.ShapeDtypeStruct(blocks.shape, BF16),
            jax.ShapeDtypeStruct(square, BF16),
        ),
        in_specs=[pl.BlockSpec(memory_space=pl.ANY)] * 3,
        out_specs=(VMEM_SPEC,) * 4,
        scratch_shapes=[
            pltpu.VMEM(basis.shape, BF16),
            pltpu.VMEM(level_transfers.shape, BF16),
            pltpu.VMEM(blocks.shape, BF16),
            pltpu.VMEM(square, BF16),
            pltpu.VMEM(square, BF16),
            pltpu.VMEM((order, 2 * order), F32),
            pltpu.VMEM((group * share, LANES), F32),
            pltpu.VMEM((pair, share, LANES), F32),
            pltpu.VMEM((group * share, LANES), F32),
            pltpu.SemaphoreType.DMA((3,)),
            pltpu.SemaphoreType.DMA((pair,)),
            pltpu.SemaphoreType.DMA((pair,)),
            pltpu.SemaphoreType.DMA((pair,)),
            pltpu.SemaphoreType.DMA((pair,)),
            pltpu.SemaphoreType.DMA((2, across)),
            pltpu.SemaphoreType.DMA((2, across)),
        ],
        compiler_params=pltpu.CompilerParams(
            vmem_limit_bytes=56 * 1024 * 1024, collective_id=0, has_side_effects=True
        ),
        cost_estimate=cost(2 * cube * 200, 4 * leaf * order),
        name="tree",
    )(basis, level_transfers, blocks)
    slot_count = blocks.shape[0]
    one = (1, order, order)
    coupled = pl.pallas_call(
        coupled_kernel,
        grid_spec=pltpu.PrefetchScalarGridSpec(
            num_scalar_prefetch=1,
            grid=(slot_count,),
            in_specs=[
                pl.BlockSpec(one, lambda k, p: (k, 0, 0)),
                pl.BlockSpec(one, lambda k, p: (p[k], 0, 0)),
            ],
            out_specs=pl.BlockSpec(one, lambda k, p: (k, 0, 0)),
        ),
        out_shape=jax.ShapeDtypeStruct(blocks.shape, BF16),
        compiler_params=BIG,
        cost_estimate=cost(4 * cube * slot_count, slot_count * order * order * 6),
        name="coupled",
    )(slots, left, gathered)
    return (q_leaf[None, None], root[None, None], coupled[None, None])


def solution(mesh):
    in_specs = (
        P("sub", "col", None, None),
        P("sub", "col", None, None, None),
        P("sub", "col", None, None, None),
        P("sub", "col", None),
    )
    out_specs = (
        P("sub", "col", None, None),
        P("sub", "col", None, None),
        P("sub", "col", None, None, None),
    )
    return jax.shard_map(shards, mesh=mesh, in_specs=in_specs, out_specs=out_specs, check_vma=False)
```
